32 devices in a mesh: day: 16 (over z, y, x), tile: 2 (over core).
Axes of the slice: x: 2, y: 2, z: 4, core: 2. Of those that a mesh axis runs over, the one named last changes fastest.
Arguments:
- library: bfloat16 [512, 2, 16384], P('day', 'tile'), may hold values from 0.05 to 24, as said below
- analog_owner: int32 [64, 30], P('day'), may hold values from 0 to 15, as said below
- analog_offset: int32 [64, 30], P('day'), may hold values from 0 to 31
- picks: int32 [64, 10, 2, 16384], P('day', None, 'tile'), may hold values from 0 to 29
- weights: bfloat16 [64, 10, 2, 16384], P('day', None, 'tile'), may hold values from 0.19921875 to 5
- target_mean: float32 [64], P('day'), may hold values from 0.5 to 5
- ranks: int32 [64, 2, 16384], P('day', 'tile'), may hold values from 0 to 99
- obs_quant: float32 [2, 100, 16384], P('tile', None, 'day'), may hold values from 0.3 to 3
- hist_quant: float32 [2, 100, 16384], P('tile', None, 'day'), may hold values from 0.5 to 2
Outputs:
- corrected: float32 [2, 64, 16384], P('tile', None, 'day')
The draws below stay inside these ranges and needn't reach their ends.
Inputs may be any that keep to these rules, and one draw needn't show every extreme that they name: `analog_owner`: among the 4 target days of one index of day (aligned blocks of rows), no owner appears more than 15 times, and in every block some owner appears exactly 15 times. `library`: Positive.
All inputs are finite; a program needn't handle non-finite values.
Results may differ from the reference program's by a relative error of at most 0.0003.
Values may be sent and summed in bfloat16 or wider, within the bound.
A program may use at most 128 MiB of HBM per device.

```python
import math
import jax
import jax.numpy as jnp
from jax import lax

CT = 16384
LD_DEV = 32
TD_DEV = 4
CANDS = 30
ANALOGS = 10
BINS = 100
CAP = 15
TILES = 2
CELLS = 32768
LD = 512
TD = 64
N_DAY = 16


def draw_library(key, part):
    key = jax.random.fold_in(key, 5)
    first, second = jax.random.split(key, 2)
    position = jnp.arange(TILES * CT, dtype=jnp.float32) / (TILES * CT)
    ramp = jnp.exp(position * math.log(3.0)).reshape(TILES, CT)
    climate = 0.2 * ramp * jnp.exp(jax.random.uniform(first, (TILES, CT), jnp.float32, 0.0, math.log(10.0)))
    daily = jnp.exp(jax.random.uniform(second, (LD, TILES, CT), jnp.float32, math.log(0.25), math.log(4.0)))
    return (climate[None] * daily).astype(jnp.bfloat16)


def draw_analog_owner(key, part):
    key = jax.random.fold_in(key, 11)
    slot_count = N_DAY * CAP
    needed = TD_DEV * CANDS

    def one_block(block_key):
        first, second, third = jax.random.split(block_key, 3)
        busiest = jax.random.randint(first, (), 0, N_DAY)
        order = jax.random.permutation(second, slot_count)
        place = jnp.argsort(order).astype(jnp.int32)
        slot_ids = jnp.arange(slot_count, dtype=jnp.int32)
        scores = jnp.where(slot_ids // CAP == busiest, slot_ids % CAP - CAP, place)
        taken = jnp.argsort(scores)[:needed].astype(jnp.int32)
        taken = jax.random.permutation(third, taken)
        return (taken // CAP).reshape(TD_DEV, CANDS)
    blocks = jax.vmap(one_block)(jax.random.split(key, N_DAY))
    return blocks.reshape(TD, CANDS).astype(jnp.int32)


def touch_ends(entries, own_key, low, high):
    longest = entries.shape.index(max(entries.shape))
    spots = []
    for shift in (0, 1):
        where = [jax.random.randint(jax.random.fold_in(own_key, axis), (), 0, length) for axis, length in enumerate(entries.shape)]
        where[longest] = (where[longest] + shift) % entries.shape[longest]
        spots.append(tuple(where))
    return entries.at[spots[0]].set(low).at[spots[1]].set(high)


def level_of(key, shape, cuts, low, top_value):
    level = 1.0
    for dim, blocks in cuts:
        draws = jax.random.uniform(jax.random.fold_in(jax.random.fold_in(key, 6), dim), (blocks,), jnp.float32, low / len(cuts), top_value / len(cuts))
        level = level * jnp.repeat(jnp.exp(draws), shape[dim] // blocks).reshape((-1,) + (1,) * (len(shape) - 1 - dim))
    return level


def setup_inputs(seed: int = 0) -> dict:
    arg_keys = jax.random.split(jax.random.key(seed), 10)
    library = draw_library(jax.random.fold_in(arg_keys[9], 71), 0)
    analog_owner = draw_analog_owner(jax.random.fold_in(arg_keys[9], 71), 0)
    analog_offset = touch_ends(jax.random.randint(arg_keys[2], (TD, CANDS), 0, LD_DEV), jax.random.fold_in(arg_keys[2], 1), 0, LD_DEV - 1).astype(jnp.int32)
    picks = touch_ends(jax.random.randint(arg_keys[3], (TD, ANALOGS, TILES, CT), 0, CANDS), jax.random.fold_in(arg_keys[3], 1), 0, CANDS - 1).astype(jnp.int32)
    weights = jnp.clip(jnp.exp(math.log(5.0) - 3.2227897 * jax.random.uniform(arg_keys[4], (TD, ANALOGS, TILES, CT), jnp.float32) ** level_of(arg_keys[4], (TD, ANALOGS, TILES, CT), ((0, 16), (2, 2)), -0.2, 0.2)), 0.19921875, 5.0).astype(jnp.bfloat16)
    target_mean = jnp.clip(jnp.exp(math.log(5.0) - 2.3025851 * jax.random.uniform(arg_keys[5], (TD,), jnp.float32) ** level_of(arg_keys[5], (TD,), ((0, 16),), -0.2, 0.2)), 0.5, 5.0)
    ranks = touch_ends(jax.random.randint(arg_keys[6], (TD, TILES, CT), 0, BINS), jax.random.fold_in(arg_keys[6], 1), 0, BINS - 1).astype(jnp.int32)
    obs_quant = jnp.clip(jnp.exp(math.log(3.0) - 2.3025851 * jax.random.uniform(arg_keys[7], (TILES, BINS, CT), jnp.float32) ** level_of(arg_keys[7], (TILES, BINS, CT), ((0, 2), (2, 16)), -0.2, 0.2)), 0.3, 3.0)
    hist_quant = jnp.clip(jnp.exp(math.log(2.0) - 1.3862944 * jax.random.uniform(arg_keys[8], (TILES, BINS, CT), jnp.float32) ** level_of(arg_keys[8], (TILES, BINS, CT), ((0, 2), (2, 16)), -0.2, 0.2)), 0.5, 2.0)
    return dict(library=library, analog_owner=analog_owner, analog_offset=analog_offset, picks=picks, weights=weights, target_mean=target_mean, ranks=ranks, obs_quant=obs_quant, hist_quant=hist_quant)


def reference(library, analog_owner, analog_offset, picks, weights, target_mean, ranks, obs_quant, hist_quant):
    day_list = (analog_owner * LD_DEV + analog_offset).astype(jnp.int32)

    def one_target(inputs):
        chosen_days, pick_rows, weight_rows = inputs
        fields = library[chosen_days]
        chosen = jnp.take_along_axis(fields, pick_rows, axis=0).astype(jnp.float32)
        weight_float = weight_rows.astype(jnp.float32)
        return jnp.sum(weight_float * chosen, axis=0) / jnp.sum(weight_float, axis=0)

    combined = lax.map(one_target, (day_list, picks, weights))
    total = jnp.sum(combined, axis=(1, 2))
    value = combined * (target_mean * CELLS / total)[:, None, None]
    ratio = obs_quant / hist_quant
    factor = jnp.take_along_axis(ratio, jnp.transpose(ranks, (1, 0, 2)), axis=1)
    return jnp.transpose(value, (1, 0, 2)) * factor
```

```python
import functools

import jax
import jax.numpy as jnp
from jax import lax
from jax.experimental import pallas as pl
from jax.experimental.pallas import tpu as pltpu
from jax.sharding import PartitionSpec as P

SLOTS = 32
HALVES = 2
LANES = 128


def pick_rows(read, groups, index):
    low = index & 7
    high = index >> 3
    out = jnp.take_along_axis(read(0), low, axis=0)
    for group in range(1, groups):
        part = jnp.take_along_axis(read(group), low, axis=0)
        out = jnp.where(high == group, part, out)
    return out


def kernel(
    sizes, lib, picks, weights, ranks, info, obs, hist, out,
    picks_in, weights_in, ranks_in, lib_recv, pw_send, pw_recv, rank_send, rank_recv,
    info_recv, rank_rows, prod, wts, comb, comb_in, sums_send, sums_recv, scale, table,
    local_sem, pick_sem, rank_sem, lib_ss, lib_rs, pw_ss, pw_rs, rk_ss, rk_rs,
    info_ss, info_rs, sum_ss, sum_rs, comb_ss, comb_rs,
):
    blocks, tiles, days, targets, analogs, cells = sizes
    group = blocks // HALVES
    total = blocks * tiles
    count = targets * analogs
    near = group * targets
    me = lax.axis_index("day")
    tile = lax.axis_index("tile")
    mine = me * tiles + tile
    half = me // group
    place = lax.rem(me, group)

    def columns(chunk):
        return pl.ds(pl.multiple_of(chunk * cells, LANES), cells)

    def pick_copy(r):
        return pltpu.make_async_copy(picks.at[r, 0], picks_in.at[r], pick_sem.at[r])

    def rank_copy(r):
        return pltpu.make_async_copy(ranks.at[r, 0], ranks_in.at[r], rank_sem.at[r])

    weight_copy = pltpu.make_async_copy(weights, weights_in, local_sem.at[0])
    weight_copy.start()
    lax.fori_loop(0, count, lambda r, c: (pick_copy(r).start(), c)[1], 0)
    for r in range(targets):
        rank_copy(r).start()

    barrier = pltpu.get_barrier_semaphore()

    def greet(j, c):
        peer = lax.rem(mine + j, total)
        pl.semaphore_signal(
            barrier, inc=1, device_id={"day": peer // tiles, "tile": lax.rem(peer, tiles)}
        )
        return c

    lax.fori_loop(1, total, greet, 0)
    pl.semaphore_wait(barrier, total - 1)

    def info_copy(src, peer):
        return pltpu.make_async_remote_copy(
            info, info_recv.at[src], info_ss.at[peer], info_rs.at[src], device_id={"day": peer}
        )

    def lib_copy(src, peer, m):
        return pltpu.make_async_remote_copy(
            lib.at[:, columns(lax.rem(peer, group) + group * m)],
            lib_recv.at[m, src],
            lib_ss.at[peer, m],
            lib_rs.at[src, m],
            device_id={"day": peer},
        )

    def own_copy(m):
        return pltpu.make_async_copy(
            lib.at[:, columns(place + group * m)], lib_recv.at[m, me], local_sem.at[1 + m]
        )

    def send_lib(j, c):
        peer = lax.rem(me + j, blocks)
        info_copy(me, peer).start()
        for m in range(HALVES):
            lib_copy(me, peer, m).start()
        return c

    for m in range(HALVES):
        own_copy(m).start()
    lax.fori_loop(1, blocks, send_lib, 0)
    info_recv[me] = info[...]

    def pw_copy(src, q):
        return pltpu.make_async_remote_copy(
            pw_send.at[q], pw_recv.at[src], pw_ss.at[q], pw_rs.at[src],
            device_id={"day": half * group + q},
        )

    def rank_out(src, peer):
        return pltpu.make_async_remote_copy(
            rank_send.at[peer], rank_recv.at[src], rk_ss.at[peer], rk_rs.at[src],
            device_id={"day": peer},
        )

    weight_copy.wait()
    lax.fori_loop(0, count, lambda r, c: (pick_copy(r).wait(), c)[1], 0)
    for r in range(targets):
        rank_copy(r).wait()

    def fill(q, dest):
        for m in range(HALVES):
            where = columns(q + group * m)
            for k in range(analogs):
                part = weights_in[k, :, where].astype(jnp.float32)
                for t in range(targets):
                    r = t * analogs + k
                    wts[r:r + 1, 0:cells] = part[t:t + 1]
            both = jnp.concatenate(
                [picks_in[:, where].astype(jnp.float32), wts[:, 0:cells]], axis=0
            )
            dest[:, m * cells:(m + 1) * cells] = both.astype(jnp.bfloat16)

    def send_pw(j, c):
        q = lax.rem(place + j, group)
        fill(q, pw_send.at[q])
        pw_copy(place, q).start()
        return c

    lax.fori_loop(1, group, send_pw, 0)
    fill(place, pw_recv.at[place])

    def send_rank(j, c):
        peer = lax.rem(me + j, blocks)
        rank_send[peer] = ranks_in[:, columns(peer)].astype(jnp.float32).astype(jnp.bfloat16)
        rank_out(me, peer).start()
        return c

    lax.fori_loop(1, blocks, send_rank, 0)
    rank_recv[me] = ranks_in[:, columns(me)].astype(jnp.float32).astype(jnp.bfloat16)

    bins = obs.shape[0]
    table[0:bins, :] = obs[...] / hist[...]
    if table.shape[0] > bins:
        table[bins:, :] = jnp.zeros((table.shape[0] - bins, cells), jnp.float32)

    def got_lib(j, c):
        src = lax.rem(me + blocks - j, blocks)
        info_copy(src, src).wait_recv()
        for m in range(HALVES):
            lib_copy(src, src, m).wait_recv()
        return c

    for m in range(HALVES):
        own_copy(m).wait()
    lax.fori_loop(1, blocks, got_lib, 0)

    day_ids = lax.broadcasted_iota(jnp.int32, (blocks * days, targets * SLOTS), 0)
    sub = lax.broadcasted_iota(jnp.int32, (8, cells), 0)

    def combine(s):
        wanted = info_recv[half * group + s][0:1, :].astype(jnp.int32)
        hot = (day_ids == wanted).astype(jnp.float32).astype(jnp.bfloat16)
        both = pw_recv[s].astype(jnp.float32)
        wts[...] = both[count:]
        for m in range(HALVES):
            fields = lax.dot_general(
                hot, lib_recv[m].reshape(blocks * days, cells),
                (((0,), (0,)), ((), ())), preferred_element_type=jnp.float32,
            )
            span = slice(m * cells, (m + 1) * cells)
            for v in range(count // 8):
                first = (8 * v) // analogs
                last = (8 * v + 7) // analogs
                rows = both[8 * v:8 * v + 8, span].astype(jnp.int32)

                def reader(t):
                    return lambda g: fields[t * SLOTS + 8 * g:t * SLOTS + 8 * g + 8]

                got = pick_rows(reader(first), SLOTS // 8, rows)
                for t in range(first + 1, last + 1):
                    more = pick_rows(reader(t), SLOTS // 8, rows)
                    got = jnp.where(sub + 8 * v >= t * analogs, more, got)
                here = slice(8 * v, 8 * v + 8)
                prod[here, span] = got * both[count + 8 * v:count + 8 * v + 8, span]
        for t in range(targets):
            here = slice(t * analogs, (t + 1) * analogs)
            top = jnp.sum(prod[here, :], axis=0, keepdims=True)
            bottom = jnp.sum(wts[here, :], axis=0, keepdims=True)
            row = top / bottom
            for m in range(HALVES):
                comb[m, pl.ds(s * targets + t, 1), :] = row[:, m * cells:(m + 1) * cells]

    combine(place)

    def arrive(j, c):
        s = lax.rem(place + group - j, group)
        pw_copy(s, s).wait_recv()
        combine(s)
        return c

    lax.fori_loop(1, group, arrive, 0)

    def comb_copy(src, dest):
        return pltpu.make_async_remote_copy(
            comb.at[dest], comb_in.at[src], comb_ss.at[dest], comb_rs.at[src],
            device_id={"day": dest * group + place},
        )

    for j in range(1, HALVES):
        comb_copy(half, lax.rem(half + j, HALVES)).start()

    width = min(near, LANES)
    square = (width, LANES)
    diagonal = lax.broadcasted_iota(jnp.int32, square, 0) == lax.broadcasted_iota(
        jnp.int32, square, 1
    )
    sums_send[...] = jnp.zeros(sums_send.shape, jnp.float32)
    for b in range(near // width):
        col = jnp.zeros((width, 1), jnp.float32)
        for m in range(HALVES):
            col += jnp.sum(comb[m, b * width:(b + 1) * width, :], axis=1, keepdims=True)
        sums_send[b:b + 1, :] = jnp.sum(
            jnp.where(diagonal, jnp.broadcast_to(col, square), 0.0), axis=0, keepdims=True
        )

    def sum_copy(src, peer):
        return pltpu.make_async_remote_copy(
            sums_send, sums_recv.at[src], sum_ss.at[peer], sum_rs.at[src],
            device_id={"day": peer // tiles, "tile": lax.rem(peer, tiles)},
        )

    lax.fori_loop(
        1, total, lambda j, c: (sum_copy(mine, lax.rem(mine + j, total)).start(), c)[1], 0
    )
    sums_recv[mine] = sums_send[...]

    def unpack(src):
        part = rank_recv[src].astype(jnp.float32).astype(jnp.int32)
        means = info_recv[src]
        for t in range(targets):
            rank_rows[pl.ds(src * targets + t, 1), :] = part[t:t + 1]
            scale[pl.ds(src * targets + t, 1), :] = means[4 + t:5 + t]

    unpack(me)

    def got_rank(j, c):
        src = lax.rem(me + blocks - j, blocks)
        rank_out(src, src).wait_recv()
        unpack(src)
        return c

    lax.fori_loop(1, blocks, got_rank, 0)
    lax.fori_loop(
        1, total,
        lambda j, c: (sum_copy(lax.rem(mine + total - j, total), 0).wait_recv(), c)[1], 0,
    )
    side = group * tiles
    for h in range(HALVES):
        acc = jnp.sum(sums_recv[h * side:(h + 1) * side], axis=0)
        for b in range(near // width):
            col = jnp.sum(
                jnp.where(diagonal, jnp.broadcast_to(acc[b:b + 1], square), 0.0),
                axis=1, keepdims=True,
            )
            here = slice(h * near + b * width, h * near + (b + 1) * width)
            scale[here, :] = scale[here, :] * float(cells * total) / col

    def finish(h, ref):
        def block(i, c):
            row = pl.multiple_of(h * near + 8 * i, 8)
            index = rank_rows[pl.ds(row, 8), :]
            factor = pick_rows(
                lambda g: table[8 * g:8 * g + 8, :], table.shape[0] // 8, index
            )
            value = ref[pl.ds(pl.multiple_of(8 * i, 8), 8), :] * scale[pl.ds(row, 8), :][:, 0:1]
            out[pl.ds(row, 8), :] = value * factor
            return c

        lax.fori_loop(0, near // 8, block, 0)

    finish(half, comb.at[half])
    for j in range(1, HALVES):
        src = lax.rem(half + j, HALVES)
        comb_copy(src, src).wait_recv()
        finish(src, comb_in.at[src])

    def drain(j, c):
        peer = lax.rem(me + j, blocks)
        info_copy(me, peer).wait_send()
        rank_out(me, peer).wait_send()
        for m in range(HALVES):
            lib_copy(me, peer, m).wait_send()
        return c

    lax.fori_loop(1, blocks, drain, 0)
    lax.fori_loop(
        1, group, lambda j, c: (pw_copy(place, lax.rem(place + j, group)).wait_send(), c)[1], 0
    )
    lax.fori_loop(
        1, total, lambda j, c: (sum_copy(mine, lax.rem(mine + j, total)).wait_send(), c)[1], 0
    )
    for j in range(1, HALVES):
        comb_copy(half, lax.rem(half + j, HALVES)).wait_send()


def per_device(
    library, analog_owner, analog_offset, picks, weights, target_mean, ranks, obs_quant, hist_quant
):
    blocks = lax.axis_size("day")
    tiles = lax.axis_size("tile")
    days = library.shape[0]
    targets, cands = analog_owner.shape
    analogs = picks.shape[1]
    cell_count = library.shape[2]
    cells = cell_count // blocks
    total_days = blocks * targets
    total = blocks * tiles
    group = blocks // HALVES
    near = group * targets
    count = targets * analogs
    bins = obs_quant.shape[1]
    padded = (bins + 7) // 8 * 8
    wide = HALVES * cells
    bf, f32, i32 = jnp.bfloat16, jnp.float32, jnp.int32

    day_list = (analog_owner * days + analog_offset).astype(f32)
    row = jnp.pad(day_list, ((0, 0), (0, SLOTS - cands))).reshape(1, targets * SLOTS)
    info = jnp.concatenate(
        [
            row,
            jnp.zeros((3, LANES), f32),
            jnp.broadcast_to(target_mean[:, None], (targets, LANES)),
        ],
        axis=0,
    )
    hbm = pl.BlockSpec(memory_space=pl.ANY)
    vmem = pl.BlockSpec(memory_space=pltpu.VMEM)
    dma = pltpu.SemaphoreType.DMA
    result = pl.pallas_call(
        functools.partial(kernel, (blocks, tiles, days, targets, analogs, cells)),
        out_shape=jax.ShapeDtypeStruct((total_days, cells), f32),
        in_specs=[hbm, hbm, hbm, hbm, vmem, vmem, vmem],
        out_specs=vmem,
        scratch_shapes=[
            pltpu.VMEM((count, cell_count), i32),
            pltpu.VMEM((analogs, targets, cell_count), bf),
            pltpu.VMEM((targets, cell_count), i32),
            pltpu.VMEM((HALVES, blocks, days, cells), bf),
            pltpu.VMEM((group, 2 * count, wide), bf),
            pltpu.VMEM((group, 2 * count, wide), bf),
            pltpu.VMEM((blocks, targets, cells), bf),
            pltpu.VMEM((blocks, targets, cells), bf),
            pltpu.VMEM((blocks, 8, LANES), f32),
            pltpu.VMEM((total_days, cells), i32),
            pltpu.VMEM((count, wide), f32),
            pltpu.VMEM((count, wide), f32),
            pltpu.VMEM((HALVES, near, cells), f32),
            pltpu.VMEM((HALVES, near, cells), f32),
            pltpu.VMEM((8, LANES), f32),
            pltpu.VMEM((total, 8, LANES), f32),
            pltpu.VMEM((total_days, LANES), f32),
            pltpu.VMEM((padded, cells), f32),
            dma((1 + HALVES,)),
            dma((count,)),
            dma((targets,)),
            dma((blocks, HALVES)),
            dma((blocks, HALVES)),
            dma((group,)),
            dma((group,)),
            dma((blocks,)),
            dma((blocks,)),
            dma((blocks,)),
            dma((blocks,)),
            dma((total,)),
            dma((total,)),
            dma((HALVES,)),
            dma((HALVES,)),
        ],
        compiler_params=pltpu.CompilerParams(
            collective_id=0, has_side_effects=True, vmem_limit_bytes=48 * 1024 * 1024
        ),
    )(
        library[:, 0],
        picks.reshape(count, 1, cell_count),
        weights[:, :, 0].transpose(1, 0, 2),
        ranks,
        info,
        obs_quant[0],
        hist_quant[0],
    )
    return result[None]


def solution(mesh):
    return jax.shard_map(
        per_device,
        mesh=mesh,
        in_specs=(
            P("day", "tile", None),
            P("day", None),
            P("day", None),
            P("day", None, "tile", None),
            P("day", None, "tile", None),
            P("day"),
            P("day", "tile", None),
            P("tile", None, "day"),
            P("tile", None, "day"),
        ),
        out_specs=P("tile", None, "day"),
        check_vma=False,
    )
```

```python
import functools

import jax
import jax.numpy as jnp
from jax import lax
from jax.experimental import pallas as pl
from jax.experimental.pallas import tpu as pltpu
from jax.sharding import PartitionSpec as P

SLOTS = 32
HALVES = 2
LANES = 128
LEAD = 3
PACE = 3


def pick_rows(read, groups, index):
    low = index & 7
    high = index >> 3
    out = jnp.take_along_axis(read(0), low, axis=0)
    for group in range(1, groups):
        part = jnp.take_along_axis(read(group), low, axis=0)
        out = jnp.where(high == group, part, out)
    return out


def kernel(
    sizes, lib, picks, weights, ranks, owner, offset, means_in, obs, hist, out,
    picks_in, weights_in, ranks_in, lib_recv, pw_send, pw_recv, rank_send, rank_recv,
    info_recv, rank_rows, prod, wts, comb, comb_in, sums_send, sums_recv, scale, table,
    info, obs_in, hist_in, table_sem,
    local_sem, pick_sem, rank_sem, lib_ss, lib_rs, pw_ss, pw_rs, rk_ss, rk_rs,
    info_ss, info_rs, sum_ss, sum_rs, comb_ss, comb_rs,
):
    blocks, tiles, days, targets, analogs, cells = sizes
    group = blocks // HALVES
    total = blocks * tiles
    count = targets * analogs
    near = group * targets
    me = lax.axis_index("day")
    tile = lax.axis_index("tile")
    mine = me * tiles + tile
    half = me // group
    place = lax.rem(me, group)

    def columns(chunk):
        return pl.ds(pl.multiple_of(chunk * cells, LANES), cells)

    def pick_copy(r):
        return pltpu.make_async_copy(picks.at[r, 0], picks_in.at[r], pick_sem.at[r])

    def rank_copy(r):
        return pltpu.make_async_copy(ranks.at[r, 0], ranks_in.at[r], rank_sem.at[r])

    weight_copy = pltpu.make_async_copy(weights, weights_in, local_sem.at[0])
    weight_copy.start()
    lax.fori_loop(0, count, lambda r, c: (pick_copy(r).start(), c)[1], 0)
    for r in range(targets):
        rank_copy(r).start()

    barrier = pltpu.get_barrier_semaphore()

    def greet(j, c):
        peer = lax.rem(mine + j, total)
        pl.semaphore_signal(
            barrier, inc=1, device_id={"day": peer // tiles, "tile": lax.rem(peer, tiles)}
        )
        return c

    lax.fori_loop(1, total, greet, 0)
    pl.semaphore_wait(barrier, total - 1)

    def info_copy(src, peer):
        return pltpu.make_async_remote_copy(
            info, info_recv.at[src], info_ss.at[peer], info_rs.at[src], device_id={"day": peer}
        )

    def lib_copy(src, peer, m):
        return pltpu.make_async_remote_copy(
            lib.at[:, columns(lax.rem(peer, group) + group * m)],
            lib_recv.at[m, src],
            lib_ss.at[peer, m],
            lib_rs.at[src, m],
            device_id={"day": peer},
        )

    def own_copy(m):
        return pltpu.make_async_copy(
            lib.at[:, columns(place + group * m)], lib_recv.at[m, me], local_sem.at[1 + m]
        )

    def send_lib(i, c):
        turn = i // (blocks - 1)
        peer = lax.rem(me + 1 + lax.rem(i, blocks - 1), blocks)
        lib_copy(me, peer, lax.rem(peer // group + 1 + turn, HALVES)).start()
        return c

    lax.fori_loop(0, LEAD, send_lib, 0)
    for m in range(HALVES):
        own_copy(m).start()
    lists = owner[...] * days + offset[...]
    info[...] = jnp.zeros(info.shape, jnp.float32)
    for t in range(targets):
        info[0:1, t * SLOTS:t * SLOTS + owner.shape[1]] = lists[t:t + 1].astype(jnp.float32)
        info[4 + t:5 + t, :] = jnp.broadcast_to(means_in[0:1, t:t + 1], (1, LANES))
    info_recv[me] = info[...]

    def send_info(j, c):
        info_copy(me, lax.rem(me + j, blocks)).start()
        return c

    lax.fori_loop(1, blocks, send_info, 0)

    def pw_copy(src, q, m):
        return pltpu.make_async_remote_copy(
            pw_send.at[m, q], pw_recv.at[m, src], pw_ss.at[m, q], pw_rs.at[m, src],
            device_id={"day": half * group + q},
        )

    def rank_out(src, peer):
        return pltpu.make_async_remote_copy(
            rank_send.at[peer], rank_recv.at[src], rk_ss.at[peer], rk_rs.at[src],
            device_id={"day": peer},
        )

    weight_copy.wait()
    lax.fori_loop(0, count, lambda r, c: (pick_copy(r).wait(), c)[1], 0)
    for r in range(targets):
        rank_copy(r).wait()

    def fill(q, m, dest):
        where = columns(q + group * m)
        for k in range(analogs):
            part = weights_in[k, :, where].astype(jnp.float32)
            for t in range(targets):
                r = t * analogs + k
                wts[r:r + 1, :] = part[t:t + 1]
        both = jnp.concatenate([picks_in[:, where].astype(jnp.float32), wts[...]], axis=0)
        dest[...] = both.astype(jnp.bfloat16)

    def turn_of(turn):
        return lax.rem(half + 1 + turn, HALVES)

    def send_pw(i, c):
        m = turn_of(i // (group - 1))
        q = lax.rem(place + 1 + lax.rem(i, group - 1), group)
        fill(q, m, pw_send.at[m, q])
        pw_copy(place, q, m).start()
        last = HALVES * (blocks - 1)
        lax.fori_loop(
            jnp.minimum(LEAD + PACE * i, last), jnp.minimum(LEAD + PACE * (i + 1), last), send_lib, 0
        )
        return c

    steps = HALVES * (group - 1)
    lax.fori_loop(0, steps, send_pw, 0)
    lax.fori_loop(
        min(LEAD + PACE * steps, HALVES * (blocks - 1)), HALVES * (blocks - 1), send_lib, 0
    )
    for m in range(HALVES):
        fill(place, m, pw_recv.at[m, place])

    def send_rank(j, c):
        peer = lax.rem(me + j, blocks)
        rank_send[peer] = ranks_in[:, columns(peer)].astype(jnp.float32).astype(jnp.bfloat16)
        rank_out(me, peer).start()
        return c

    lax.fori_loop(1, blocks, send_rank, 0)
    rank_recv[me] = ranks_in[:, columns(me)].astype(jnp.float32).astype(jnp.bfloat16)

    bins = obs.shape[0]

    def table_copies(r):
        return (
            pltpu.make_async_copy(obs.at[r, 0], obs_in.at[r], table_sem.at[0, r]),
            pltpu.make_async_copy(hist.at[r, 0], hist_in.at[r], table_sem.at[1, r]),
        )

    lax.fori_loop(0, bins, lambda r, c: ([x.start() for x in table_copies(r)], c)[1], 0)
    lax.fori_loop(0, bins, lambda r, c: ([x.wait() for x in table_copies(r)], c)[1], 0)
    table[0:bins, :] = obs_in[...] / hist_in[...]
    if table.shape[0] > bins:
        table[bins:, :] = jnp.zeros((table.shape[0] - bins, cells), jnp.float32)

    def got_info(j, c):
        src = lax.rem(me + blocks - j, blocks)
        info_copy(src, src).wait_recv()
        return c

    lax.fori_loop(1, blocks, got_info, 0)
    day_ids = lax.broadcasted_iota(jnp.int32, (blocks * days, targets * SLOTS), 0)
    sub = lax.broadcasted_iota(jnp.int32, (8, cells), 0)

    def combine(s, m):
        wanted = info_recv[half * group + s][0:1, :].astype(jnp.int32)
        hot = (day_ids == wanted).astype(jnp.float32).astype(jnp.bfloat16)
        both = pw_recv[m, s].astype(jnp.float32)
        wts[...] = both[count:]
        fields = lax.dot_general(
            hot, lib_recv[m].reshape(blocks * days, cells),
            (((0,), (0,)), ((), ())), preferred_element_type=jnp.float32,
        )
        for v in range(count // 8):
            first = (8 * v) // analogs
            last = (8 * v + 7) // analogs
            here = slice(8 * v, 8 * v + 8)
            rows = both[here].astype(jnp.int32)

            def reader(t):
                return lambda g: fields[t * SLOTS + 8 * g:t * SLOTS + 8 * g + 8]

            got = pick_rows(reader(first), SLOTS // 8, rows)
            for t in range(first + 1, last + 1):
                more = pick_rows(reader(t), SLOTS // 8, rows)
                got = jnp.where(sub + 8 * v >= t * analogs, more, got)
            prod[here, :] = got * both[count + 8 * v:count + 8 * v + 8]
        for t in range(targets):
            here = slice(t * analogs, (t + 1) * analogs)
            top = jnp.sum(prod[here, :], axis=0, keepdims=True)
            bottom = jnp.sum(wts[here, :], axis=0, keepdims=True)
            comb[m, pl.ds(s * targets + t, 1), :] = top / bottom

    def comb_copy(src, dest):
        return pltpu.make_async_remote_copy(
            comb.at[dest], comb_in.at[src], comb_ss.at[dest], comb_rs.at[src],
            device_id={"day": dest * group + place},
        )

    for turn in range(HALVES):
        m = turn_of(turn)

        def got_lib(j, c):
            src = lax.rem(me + blocks - j, blocks)
            lib_copy(src, src, m).wait_recv()
            return c

        def arrive(j, c):
            s = lax.rem(place + group - j, group)
            pw_copy(s, s, m).wait_recv()
            combine(s, m)
            return c

        own_copy(m).wait()
        lax.fori_loop(1, blocks, got_lib, 0)
        combine(place, m)
        lax.fori_loop(1, group, arrive, 0)
        if turn < HALVES - 1:
            comb_copy(half, m).start()

    width = min(near, LANES)
    square = (width, LANES)
    diagonal = lax.broadcasted_iota(jnp.int32, square, 0) == lax.broadcasted_iota(
        jnp.int32, square, 1
    )
    sums_send[...] = jnp.zeros(sums_send.shape, jnp.float32)
    for b in range(near // width):
        col = jnp.zeros((width, 1), jnp.float32)
        for m in range(HALVES):
            col += jnp.sum(comb[m, b * width:(b + 1) * width, :], axis=1, keepdims=True)
        sums_send[b:b + 1, :] = jnp.sum(
            jnp.where(diagonal, jnp.broadcast_to(col, square), 0.0), axis=0, keepdims=True
        )

    def sum_copy(src, peer):
        return pltpu.make_async_remote_copy(
            sums_send, sums_recv.at[src], sum_ss.at[peer], sum_rs.at[src],
            device_id={"day": peer // tiles, "tile": lax.rem(peer, tiles)},
        )

    lax.fori_loop(
        1, total, lambda j, c: (sum_copy(mine, lax.rem(mine + j, total)).start(), c)[1], 0
    )
    sums_recv[mine] = sums_send[...]

    def unpack(src):
        part = rank_recv[src].astype(jnp.float32).astype(jnp.int32)
        means = info_recv[src]
        for t in range(targets):
            rank_rows[pl.ds(src * targets + t, 1), :] = part[t:t + 1]
            scale[pl.ds(src * targets + t, 1), :] = means[4 + t:5 + t]

    unpack(me)

    def got_rank(j, c):
        src = lax.rem(me + blocks - j, blocks)
        rank_out(src, src).wait_recv()
        unpack(src)
        return c

    lax.fori_loop(1, blocks, got_rank, 0)
    lax.fori_loop(
        1, total,
        lambda j, c: (sum_copy(lax.rem(mine + total - j, total), 0).wait_recv(), c)[1], 0,
    )
    side = group * tiles
    for h in range(HALVES):
        acc = jnp.sum(sums_recv[h * side:(h + 1) * side], axis=0)
        for b in range(near // width):
            col = jnp.sum(
                jnp.where(diagonal, jnp.broadcast_to(acc[b:b + 1], square), 0.0),
                axis=1, keepdims=True,
            )
            here = slice(h * near + b * width, h * near + (b + 1) * width)
            scale[here, :] = scale[here, :] * float(cells * total) / col

    def finish(h, ref):
        def block(i, c):
            row = pl.multiple_of(h * near + 8 * i, 8)
            index = rank_rows[pl.ds(row, 8), :]
            factor = pick_rows(
                lambda g: table[8 * g:8 * g + 8, :], table.shape[0] // 8, index
            )
            value = ref[pl.ds(pl.multiple_of(8 * i, 8), 8), :] * scale[pl.ds(row, 8), :][:, 0:1]
            out[pl.ds(row, 8), :] = value * factor
            return c

        lax.fori_loop(0, near // 8, block, 0)

    finish(half, comb.at[half])
    for j in range(1, HALVES):
        src = lax.rem(half + j, HALVES)
        comb_copy(src, src).wait_recv()
        finish(src, comb_in.at[src])

    def drain(j, c):
        peer = lax.rem(me + j, blocks)
        info_copy(me, peer).wait_send()
        rank_out(me, peer).wait_send()
        for m in range(HALVES):
            lib_copy(me, peer, m).wait_send()
        return c

    lax.fori_loop(1, blocks, drain, 0)
    for m in range(HALVES):
        lax.fori_loop(
            1, group,
            lambda j, c: (pw_copy(place, lax.rem(place + j, group), m).wait_send(), c)[1], 0,
        )
    lax.fori_loop(
        1, total, lambda j, c: (sum_copy(mine, lax.rem(mine + j, total)).wait_send(), c)[1], 0
    )
    for j in range(1, HALVES):
        comb_copy(half, lax.rem(half + j, HALVES)).wait_send()


def per_device(
    library, analog_owner, analog_offset, picks, weights, target_mean, ranks, obs_quant, hist_quant
):
    blocks = lax.axis_size("day")
    tiles = lax.axis_size("tile")
    days = library.shape[0]
    targets = analog_owner.shape[0]
    analogs = picks.shape[1]
    cell_count = library.shape[2]
    cells = cell_count // blocks
    total_days = blocks * targets
    total = blocks * tiles
    group = blocks // HALVES
    near = group * targets
    count = targets * analogs
    bins = obs_quant.shape[1]
    padded = (bins + 7) // 8 * 8
    bf, f32, i32 = jnp.bfloat16, jnp.float32, jnp.int32

    hbm = pl.BlockSpec(memory_space=pl.ANY)
    vmem = pl.BlockSpec(memory_space=pltpu.VMEM)
    dma = pltpu.SemaphoreType.DMA
    result = pl.pallas_call(
        functools.partial(kernel, (blocks, tiles, days, targets, analogs, cells)),
        out_shape=jax.ShapeDtypeStruct((total_days, cells), f32),
        in_specs=[hbm, hbm, hbm, hbm, vmem, vmem, vmem, hbm, hbm],
        out_specs=vmem,
        scratch_shapes=[
            pltpu.VMEM((count, cell_count), i32),
            pltpu.VMEM((analogs, targets, cell_count), bf),
            pltpu.VMEM((targets, cell_count), i32),
            pltpu.VMEM((HALVES, blocks, days, cells), bf),
            pltpu.VMEM((HALVES, group, 2 * count, cells), bf),
            pltpu.VMEM((HALVES, group, 2 * count, cells), bf),
            pltpu.VMEM((blocks, targets, cells), bf),
            pltpu.VMEM((blocks, targets, cells), bf),
            pltpu.VMEM((blocks, 8, LANES), f32),
            pltpu.VMEM((total_days, cells), i32),
            pltpu.VMEM((count, cells), f32),
            pltpu.VMEM((count, cells), f32),
            pltpu.VMEM((HALVES, near, cells), f32),
            pltpu.VMEM((HALVES, near, cells), f32),
            pltpu.VMEM((8, LANES), f32),
            pltpu.VMEM((total, 8, LANES), f32),
            pltpu.VMEM((total_days, LANES), f32),
            pltpu.VMEM((padded, cells), f32),
            pltpu.VMEM((8, LANES), f32),
            pltpu.VMEM((bins, cells), f32),
            pltpu.VMEM((bins, cells), f32),
            dma((2, bins)),
            dma((1 + HALVES,)),
            dma((count,)),
            dma((targets,)),
            dma((blocks, HALVES)),
            dma((blocks, HALVES)),
            dma((HALVES, group)),
            dma((HALVES, group)),
            dma((blocks,)),
            dma((blocks,)),
            dma((blocks,)),
            dma((blocks,)),
            dma((total,)),
            dma((total,)),
            dma((HALVES,)),
            dma((HALVES,)),
        ],
        compiler_params=pltpu.CompilerParams(
            collective_id=0, has_side_effects=True, vmem_limit_bytes=60 * 1024 * 1024
        ),
    )(
        library[:, 0],
        picks.reshape(count, 1, cell_count),
        weights[:, :, 0].transpose(1, 0, 2),
        ranks,
        analog_owner,
        analog_offset,
        target_mean.reshape(1, targets),
        obs_quant.reshape(bins, 1, cells),
        hist_quant.reshape(bins, 1, cells),
    )
    return result[None]


def solution(mesh):
    return jax.shard_map(
        per_device,
        mesh=mesh,
        in_specs=(
            P("day", "tile", None),
            P("day", None),
            P("day", None),
            P("day", None, "tile", None),
            P("day", None, "tile", None),
            P("day"),
            P("day", "tile", None),
            P("tile", None, "day"),
            P("tile", None, "day"),
        ),
        out_specs=P("tile", None, "day"),
        check_vma=False,
    )
```

```python
import functools

import jax
import jax.numpy as jnp
from jax import lax
from jax.experimental import pallas as pl
from jax.experimental.pallas import tpu as pltpu
from jax.sharding import PartitionSpec as P

SLOTS = 32
HALVES = 2
LANES = 128
LEAD = 3
PACE = 3


def pick_rows(read, groups, index):
    low = index & 7
    high = index >> 3
    out = jnp.take_along_axis(read(0), low, axis=0)
    for group in range(1, groups):
        part = jnp.take_along_axis(read(group), low, axis=0)
        out = jnp.where(high == group, part, out)
    return out


def kernel(
    sizes, lib, picks, weights, ranks, owner, offset, means_in, obs, hist, out,
    picks_in, weights_in, ranks_in, lib_recv, pw_send, pw_recv, rank_send, rank_recv,
    info_recv, rank_rows, prod, wts, comb, comb_in, sums_send, sums_recv, scale, table,
    info, obs_in, hist_in, table_sem,
    local_sem, pick_sem, rank_sem, lib_ss, lib_rs, pw_ss, pw_rs, rk_ss, rk_rs,
    info_ss, info_rs, sum_ss, sum_rs, comb_ss, comb_rs,
):
    blocks, tiles, days, targets, analogs, cells = sizes
    group = blocks // HALVES
    total = blocks * tiles
    count = targets * analogs
    near = group * targets
    me = lax.axis_index("day")
    tile = lax.axis_index("tile")
    mine = me * tiles + tile
    half = me // group
    place = lax.rem(me, group)

    def columns(chunk):
        return pl.ds(pl.multiple_of(chunk * cells, LANES), cells)

    def pick_copy(r):
        return pltpu.make_async_copy(picks.at[r, 0], picks_in.at[r], pick_sem.at[r])

    def rank_copy(r):
        return pltpu.make_async_copy(ranks.at[r, 0], ranks_in.at[r], rank_sem.at[r])

    weight_copy = pltpu.make_async_copy(weights, weights_in, local_sem.at[0])
    weight_copy.start()
    lax.fori_loop(0, count, lambda r, c: (pick_copy(r).start(), c)[1], 0)
    for r in range(targets):
        rank_copy(r).start()

    barrier = pltpu.get_barrier_semaphore()

    def greet(j, c):
        peer = lax.rem(mine + j, total)
        pl.semaphore_signal(
            barrier, inc=1, device_id={"day": peer // tiles, "tile": lax.rem(peer, tiles)}
        )
        return c

    lax.fori_loop(1, total, greet, 0)
    pl.semaphore_wait(barrier, total - 1)

    def info_copy(src, peer):
        return pltpu.make_async_remote_copy(
            info, info_recv.at[src], info_ss.at[peer], info_rs.at[src], device_id={"day": peer}
        )

    def lib_copy(src, peer, m):
        return pltpu.make_async_remote_copy(
            lib.at[:, columns(lax.rem(peer, group) + group * m)],
            lib_recv.at[m, src],
            lib_ss.at[peer, m],
            lib_rs.at[src, m],
            device_id={"day": peer},
        )

    def own_copy(m):
        return pltpu.make_async_copy(
            lib.at[:, columns(place + group * m)], lib_recv.at[m, me], local_sem.at[1 + m]
        )

    def send_lib(i, c):
        turn = i // (blocks - 1)
        away = 1 + lax.rem(i, blocks - 1)
        peer = lax.rem(me + away + tile * (blocks - 2 * away), blocks)
        lib_copy(me, peer, lax.rem(peer // group + 1 + turn, HALVES)).start()
        return c

    lax.fori_loop(0, LEAD, send_lib, 0)
    for m in range(HALVES):
        own_copy(m).start()
    lists = owner[...] * days + offset[...]
    info[...] = jnp.zeros(info.shape, jnp.float32)
    for t in range(targets):
        info[0:1, t * SLOTS:t * SLOTS + owner.shape[1]] = lists[t:t + 1].astype(jnp.float32)
        info[4 + t:5 + t, :] = jnp.broadcast_to(means_in[0:1, t:t + 1], (1, LANES))
    info_recv[me] = info[...]

    def send_info(j, c):
        info_copy(me, lax.rem(me + j, blocks)).start()
        return c

    lax.fori_loop(1, blocks, send_info, 0)

    def pw_copy(src, q, m):
        return pltpu.make_async_remote_copy(
            pw_send.at[m, q], pw_recv.at[m, src], pw_ss.at[m, q], pw_rs.at[m, src],
            device_id={"day": half * group + q},
        )

    def rank_out(src, peer):
        return pltpu.make_async_remote_copy(
            rank_send.at[peer], rank_recv.at[src], rk_ss.at[peer], rk_rs.at[src],
            device_id={"day": peer},
        )

    weight_copy.wait()
    lax.fori_loop(0, count, lambda r, c: (pick_copy(r).wait(), c)[1], 0)
    for r in range(targets):
        rank_copy(r).wait()

    def fill(q, m, dest):
        where = columns(q + group * m)
        for k in range(analogs):
            part = weights_in[k, :, where].astype(jnp.float32)
            for t in range(targets):
                r = t * analogs + k
                wts[r:r + 1, :] = part[t:t + 1]
        both = jnp.concatenate([picks_in[:, where].astype(jnp.float32), wts[...]], axis=0)
        dest[...] = both.astype(jnp.bfloat16)

    def turn_of(turn):
        return lax.rem(half + 1 + turn, HALVES)

    def send_pw(i, c):
        m = turn_of(i // (group - 1))
        away = 1 + lax.rem(i, group - 1)
        q = lax.rem(place + away + tile * (group - 2 * away), group)
        fill(q, m, pw_send.at[m, q])
        pw_copy(place, q, m).start()
        last = HALVES * (blocks - 1)
        lax.fori_loop(
            jnp.minimum(LEAD + PACE * i, last), jnp.minimum(LEAD + PACE * (i + 1), last), send_lib, 0
        )
        return c

    steps = HALVES * (group - 1)
    lax.fori_loop(0, steps, send_pw, 0)
    lax.fori_loop(
        min(LEAD + PACE * steps, HALVES * (blocks - 1)), HALVES * (blocks - 1), send_lib, 0
    )
    for m in range(HALVES):
        fill(place, m, pw_recv.at[m, place])

    def send_rank(j, c):
        peer = lax.rem(me + j, blocks)
        rank_send[peer] = ranks_in[:, columns(peer)].astype(jnp.float32).astype(jnp.bfloat16)
        rank_out(me, peer).start()
        return c

    lax.fori_loop(1, blocks, send_rank, 0)
    rank_recv[me] = ranks_in[:, columns(me)].astype(jnp.float32).astype(jnp.bfloat16)

    bins = obs.shape[0]

    def table_copies(r):
        return (
            pltpu.make_async_copy(obs.at[r, 0], obs_in.at[r], table_sem.at[0, r]),
            pltpu.make_async_copy(hist.at[r, 0], hist_in.at[r], table_sem.at[1, r]),
        )

    lax.fori_loop(0, bins, lambda r, c: ([x.start() for x in table_copies(r)], c)[1], 0)
    lax.fori_loop(0, bins, lambda r, c: ([x.wait() for x in table_copies(r)], c)[1], 0)
    table[0:bins, :] = obs_in[...] / hist_in[...]
    if table.shape[0] > bins:
        table[bins:, :] = jnp.zeros((table.shape[0] - bins, cells), jnp.float32)

    def got_info(j, c):
        src = lax.rem(me + blocks - j, blocks)
        info_copy(src, src).wait_recv()
        return c

    lax.fori_loop(1, blocks, got_info, 0)
    day_ids = lax.broadcasted_iota(jnp.int32, (blocks * days, targets * SLOTS), 0)
    sub = lax.broadcasted_iota(jnp.int32, (8, cells), 0)

    def combine(s, m):
        wanted = info_recv[half * group + s][0:1, :].astype(jnp.int32)
        hot = (day_ids == wanted).astype(jnp.float32).astype(jnp.bfloat16)
        both = pw_recv[m, s].astype(jnp.float32)
        wts[...] = both[count:]
        fields = lax.dot_general(
            hot, lib_recv[m].reshape(blocks * days, cells),
            (((0,), (0,)), ((), ())), preferred_element_type=jnp.float32,
        )
        for v in range(count // 8):
            first = (8 * v) // analogs
            last = (8 * v + 7) // analogs
            here = slice(8 * v, 8 * v + 8)
            rows = both[here].astype(jnp.int32)

            def reader(t):
                return lambda g: fields[t * SLOTS + 8 * g:t * SLOTS + 8 * g + 8]

            got = pick_rows(reader(first), SLOTS // 8, rows)
            for t in range(first + 1, last + 1):
                more = pick_rows(reader(t), SLOTS // 8, rows)
                got = jnp.where(sub + 8 * v >= t * analogs, more, got)
            prod[here, :] = got * both[count + 8 * v:count + 8 * v + 8]
        for t in range(targets):
            here = slice(t * analogs, (t + 1) * analogs)
            top = jnp.sum(prod[here, :], axis=0, keepdims=True)
            bottom = jnp.sum(wts[here, :], axis=0, keepdims=True)
            comb[m, pl.ds(s * targets + t, 1), :] = top / bottom

    def comb_copy(src, dest):
        return pltpu.make_async_remote_copy(
            comb.at[dest], comb_in.at[src], comb_ss.at[dest], comb_rs.at[src],
            device_id={"day": dest * group + place},
        )

    for turn in range(HALVES):
        m = turn_of(turn)

        def got_lib(j, c):
            src = lax.rem(me + blocks - j, blocks)
            lib_copy(src, src, m).wait_recv()
            return c

        def arrive(j, c):
            s = lax.rem(place + group - j, group)
            pw_copy(s, s, m).wait_recv()
            combine(s, m)
            return c

        own_copy(m).wait()
        lax.fori_loop(1, blocks, got_lib, 0)
        combine(place, m)
        lax.fori_loop(1, group, arrive, 0)
        if turn < HALVES - 1:
            comb_copy(half, m).start()

    width = min(near, LANES)
    square = (width, LANES)
    diagonal = lax.broadcasted_iota(jnp.int32, square, 0) == lax.broadcasted_iota(
        jnp.int32, square, 1
    )
    sums_send[...] = jnp.zeros(sums_send.shape, jnp.float32)
    for b in range(near // width):
        col = jnp.zeros((width, 1), jnp.float32)
        for m in range(HALVES):
            col += jnp.sum(comb[m, b * width:(b + 1) * width, :], axis=1, keepdims=True)
        sums_send[b:b + 1, :] = jnp.sum(
            jnp.where(diagonal, jnp.broadcast_to(col, square), 0.0), axis=0, keepdims=True
        )

    def sum_copy(src, peer):
        return pltpu.make_async_remote_copy(
            sums_send, sums_recv.at[src], sum_ss.at[peer], sum_rs.at[src],
            device_id={"day": peer // tiles, "tile": lax.rem(peer, tiles)},
        )

    lax.fori_loop(
        1, total, lambda j, c: (sum_copy(mine, lax.rem(mine + j, total)).start(), c)[1], 0
    )
    sums_recv[mine] = sums_send[...]

    def unpack(src):
        part = rank_recv[src].astype(jnp.float32).astype(jnp.int32)
        means = info_recv[src]
        for t in range(targets):
            rank_rows[pl.ds(src * targets + t, 1), :] = part[t:t + 1]
            scale[pl.ds(src * targets + t, 1), :] = means[4 + t:5 + t]

    unpack(me)

    def got_rank(j, c):
        src = lax.rem(me + blocks - j, blocks)
        rank_out(src, src).wait_recv()
        unpack(src)
        return c

    lax.fori_loop(1, blocks, got_rank, 0)
    lax.fori_loop(
        1, total,
        lambda j, c: (sum_copy(lax.rem(mine + total - j, total), 0).wait_recv(), c)[1], 0,
    )
    side = group * tiles
    for h in range(HALVES):
        acc = jnp.sum(sums_recv[h * side:(h + 1) * side], axis=0)
        for b in range(near // width):
            col = jnp.sum(
                jnp.where(diagonal, jnp.broadcast_to(acc[b:b + 1], square), 0.0),
                axis=1, keepdims=True,
            )
            here = slice(h * near + b * width, h * near + (b + 1) * width)
            scale[here, :] = scale[here, :] * float(cells * total) / col

    def finish(h, ref):
        def block(i, c):
            row = pl.multiple_of(h * near + 8 * i, 8)
            index = rank_rows[pl.ds(row, 8), :]
            factor = pick_rows(
                lambda g: table[8 * g:8 * g + 8, :], table.shape[0] // 8, index
            )
            value = ref[pl.ds(pl.multiple_of(8 * i, 8), 8), :] * scale[pl.ds(row, 8), :][:, 0:1]
            out[pl.ds(row, 8), :] = value * factor
            return c

        lax.fori_loop(0, near // 8, block, 0)

    finish(half, comb.at[half])
    for j in range(1, HALVES):
        src = lax.rem(half + j, HALVES)
        comb_copy(src, src).wait_recv()
        finish(src, comb_in.at[src])

    def drain(j, c):
        peer = lax.rem(me + j, blocks)
        info_copy(me, peer).wait_send()
        rank_out(me, peer).wait_send()
        for m in range(HALVES):
            lib_copy(me, peer, m).wait_send()
        return c

    lax.fori_loop(1, blocks, drain, 0)
    for m in range(HALVES):
        lax.fori_loop(
            1, group,
            lambda j, c: (pw_copy(place, lax.rem(place + j, group), m).wait_send(), c)[1], 0,
        )
    lax.fori_loop(
        1, total, lambda j, c: (sum_copy(mine, lax.rem(mine + j, total)).wait_send(), c)[1], 0
    )
    for j in range(1, HALVES):
        comb_copy(half, lax.rem(half + j, HALVES)).wait_send()


def per_device(
    library, analog_owner, analog_offset, picks, weights, target_mean, ranks, obs_quant, hist_quant
):
    blocks = lax.axis_size("day")
    tiles = lax.axis_size("tile")
    days = library.shape[0]
    targets = analog_owner.shape[0]
    analogs = picks.shape[1]
    cell_count = library.shape[2]
    cells = cell_count // blocks
    total_days = blocks * targets
    total = blocks * tiles
    group = blocks // HALVES
    near = group * targets
    count = targets * analogs
    bins = obs_quant.shape[1]
    padded = (bins + 7) // 8 * 8
    bf, f32, i32 = jnp.bfloat16, jnp.float32, jnp.int32

    hbm = pl.BlockSpec(memory_space=pl.ANY)
    vmem = pl.BlockSpec(memory_space=pltpu.VMEM)
    dma = pltpu.SemaphoreType.DMA
    result = pl.pallas_call(
        functools.partial(kernel, (blocks, tiles, days, targets, analogs, cells)),
        out_shape=jax.ShapeDtypeStruct((total_days, cells), f32),
        in_specs=[hbm, hbm, hbm, hbm, vmem, vmem, vmem, hbm, hbm],
        out_specs=vmem,
        scratch_shapes=[
            pltpu.VMEM((count, cell_count), i32),
            pltpu.VMEM((analogs, targets, cell_count), bf),
            pltpu.VMEM((targets, cell_count), i32),
            pltpu.VMEM((HALVES, blocks, days, cells), bf),
            pltpu.VMEM((HALVES, group, 2 * count, cells), bf),
            pltpu.VMEM((HALVES, group, 2 * count, cells), bf),
            pltpu.VMEM((blocks, targets, cells), bf),
            pltpu.VMEM((blocks, targets, cells), bf),
            pltpu.VMEM((blocks, 8, LANES), f32),
            pltpu.VMEM((total_days, cells), i32),
            pltpu.VMEM((count, cells), f32),
            pltpu.VMEM((count, cells), f32),
            pltpu.VMEM((HALVES, near, cells), f32),
            pltpu.VMEM((HALVES, near, cells), f32),
            pltpu.VMEM((8, LANES), f32),
            pltpu.VMEM((total, 8, LANES), f32),
            pltpu.VMEM((total_days, LANES), f32),
            pltpu.VMEM((padded, cells), f32),
            pltpu.VMEM((8, LANES), f32),
            pltpu.VMEM((bins, cells), f32),
            pltpu.VMEM((bins, cells), f32),
            dma((2, bins)),
            dma((1 + HALVES,)),
            dma((count,)),
            dma((targets,)),
            dma((blocks, HALVES)),
            dma((blocks, HALVES)),
            dma((HALVES, group)),
            dma((HALVES, group)),
            dma((blocks,)),
            dma((blocks,)),
            dma((blocks,)),
            dma((blocks,)),
            dma((total,)),
            dma((total,)),
            dma((HALVES,)),
            dma((HALVES,)),
        ],
        compiler_params=pltpu.CompilerParams(
            collective_id=0, has_side_effects=True, vmem_limit_bytes=60 * 1024 * 1024
        ),
    )(
        library[:, 0],
        picks.reshape(count, 1, cell_count),
        weights[:, :, 0].transpose(1, 0, 2),
        ranks,
        analog_owner,
        analog_offset,
        target_mean.reshape(1, targets),
        obs_quant.reshape(bins, 1, cells),
        hist_quant.reshape(bins, 1, cells),
    )
    return result[None]


def solution(mesh):
    return jax.shard_map(
        per_device,
        mesh=mesh,
        in_specs=(
            P("day", "tile", None),
            P("day", None),
            P("day", None),
            P("day", None, "tile", None),
            P("day", None, "tile", None),
            P("day"),
            P("day", "tile", None),
            P("tile", None, "day"),
            P("tile", None, "day"),
        ),
        out_specs=P("tile", None, "day"),
        check_vma=False,
    )
```
